128 devices in a mesh: grp: 8 (over z, core), tile: 16 (over y, x).
Axes of the slice: x: 4, y: 4, z: 4, core: 2. Of those that a mesh axis runs over, the one named last changes fastest.
Arguments:
- embeddings: bfloat16 [49152, 1024], P(('grp', 'tile'))
- row_group: int32 [49152], P(('grp', 'tile')), may hold values from 0 to 7, as said below
- row_cluster: int32 [49152], P(('grp', 'tile')), may hold values from 0 to 1
Outputs:
- best_match: float32 [49152], P(('grp', 'tile'))
The draws below stay inside these ranges and needn't reach their ends.
Inputs may be any that keep to these rules, and one draw needn't show every extreme that they name: `row_group`: among the rows of one device no group is named by more than 96 rows; for every index along tile some group is named by exactly 96 rows on every device of that tile index.
All inputs are finite; a program needn't handle non-finite values.
Results may differ from the reference program's by a relative error of at most 0.00053.
Values may be sent and summed in bfloat16 or wider, within the bound.
No kernel may reach another device: no remote copies, remote signals or barrier semaphores. Data moves between devices by JAX's collectives and lax.ppermute only.
A program may use at most 128 MiB of HBM per device.

```python
from functools import partial
import jax
import jax.numpy as jnp
from jax import lax

D = 1024
ROWS_DEV = 384
CL_GRP = 2
GROUPS = 8
TILES = 16
CAP = 96
ROWS = 49152


def assign_rows(key):
    key_busy, key_rank, key_order, key_cuts, key_cluster = jax.random.split(key, 5)
    block_count = GROUPS * TILES
    busiest = jnp.tile(jax.random.randint(key_busy, (TILES,), 0, GROUPS), GROUPS)
    ranking = jax.vmap(lambda single: jax.random.permutation(single, ROWS_DEV))(jax.random.split(key_rank, block_count))
    ordering = jax.vmap(lambda single: jax.random.permutation(single, GROUPS - 1))(jax.random.split(key_order, block_count))
    remaining = ROWS_DEV - CAP
    jitter = CAP // 8
    centres = jnp.arange(1, GROUPS - 1, dtype=jnp.int32) * remaining // (GROUPS - 1)
    cutoff = centres[None, :] + jax.random.randint(key_cuts, (block_count, GROUPS - 2), -jitter, jitter + 1)
    past_busy = ranking - CAP
    pieces = jnp.sum((past_busy[:, :, None] >= cutoff[:, None, :]).astype(jnp.int32), axis=2)
    others = (busiest[:, None] + 1 + jnp.take_along_axis(ordering, pieces, axis=1)) % GROUPS
    owners = jnp.where(ranking < CAP, busiest[:, None], others).reshape(ROWS).astype(jnp.int32)
    cluster = jax.random.randint(key_cluster, (ROWS,), 0, CL_GRP).astype(jnp.int32)
    return (owners, cluster)


def draw_row_group(key, part):
    owners, cluster = assign_rows(key)
    return owners


def draw_row_cluster(key, part):
    owners, cluster = assign_rows(key)
    return cluster


def draw_embeddings(key, part):
    owners, cluster = assign_rows(key)
    key = jax.random.fold_in(key, 11)
    key_noise, key_ties, key_mix = jax.random.split(key, 3)
    cluster_key = owners * CL_GRP + cluster
    tie_break = jax.random.permutation(key_ties, ROWS).astype(jnp.int32)
    sorting = jnp.argsort(cluster_key * ROWS + tie_break, stable=True).astype(jnp.int32)
    previous = jnp.concatenate([sorting[:1], sorting[:-1]])
    partner_sorted = jnp.where(cluster_key[previous] == cluster_key[sorting], previous, sorting)
    partner = jnp.zeros((ROWS,), jnp.int32).at[sorting].set(partner_sorted.astype(jnp.int32))
    mixing = jnp.exp(jax.random.uniform(key_mix, (ROWS, 1), jnp.float32, jnp.log(0.2), jnp.log(4.0)))
    base_noise = jnp.clip(jax.random.normal(key_noise, (ROWS, D), jnp.float32), -6.0, 6.0)
    values = base_noise + mixing * base_noise[partner]
    return values.astype(jnp.bfloat16)


def setup_inputs(seed: int = 0) -> dict:
    seeds = jax.random.split(jax.random.key(seed), 4)
    return {
        "embeddings": draw_embeddings(jax.random.fold_in(seeds[3], 71), 0),
        "row_group": draw_row_group(jax.random.fold_in(seeds[3], 71), 0),
        "row_cluster": draw_row_cluster(jax.random.fold_in(seeds[3], 71), 0),
    }


epsilon = 1e-06

def unit_rows(values):
    floats = values.astype(jnp.float32)
    scaled = floats * lax.rsqrt(lax.optimization_barrier(jnp.sum(floats * floats, axis=-1, keepdims=True)) + epsilon)
    return scaled.astype(jnp.bfloat16)

def slot_index(owners, groups, capacity):
    onehot = (owners[:, None] == jnp.arange(groups, dtype=jnp.int32)[None, :]).astype(jnp.int32)
    earlier = jnp.cumsum(onehot, axis=0) - onehot
    ranked = lax.optimization_barrier(jnp.sum(earlier * onehot, axis=1))
    return (owners * capacity + ranked).astype(jnp.int32)

def masked_table(scores, left_ids, right_ids, left_pos, right_pos):
    allowed = (left_ids[:, None] == right_ids[None, :]) & (right_ids[None, :] >= 0) & (left_pos[:, None] != right_pos[None, :])
    return jnp.where(allowed, scores, jnp.float32(-1.0))

def fill_slots(normed, where_to, cluster_tags):
    buffer = jnp.zeros((GROUPS * CAP, D), jnp.bfloat16).at[where_to].set(normed)
    tagged = jnp.full((GROUPS * CAP,), -1, jnp.int32).at[where_to].set(cluster_tags)
    return (buffer, tagged)

def reference(embeddings, row_group, row_cluster):
    blocks = GROUPS * TILES
    slots_all = GROUPS * CAP
    normed = unit_rows(embeddings).reshape(blocks, ROWS_DEV, D)
    owners = row_group.reshape(blocks, ROWS_DEV)
    labels = row_cluster.reshape(blocks, ROWS_DEV)
    placed = jax.vmap(partial(slot_index, groups=GROUPS, capacity=CAP))(owners)
    buffers, tagged = jax.vmap(fill_slots)(normed, placed, labels)
    buffers = buffers.reshape(GROUPS, TILES, GROUPS, CAP, D).transpose(2, 1, 0, 3, 4).reshape(GROUPS, TILES * slots_all, D)
    tagged = tagged.reshape(GROUPS, TILES, GROUPS, CAP).transpose(2, 1, 0, 3).reshape(GROUPS, TILES * slots_all)
    positions = jnp.arange(TILES * slots_all, dtype=jnp.int32)

    def per_group(operands):
        members, member_ids = operands
        floats = members.astype(jnp.float32)

        def per_tile(tile_index):
            first_row = (tile_index * slots_all).astype(jnp.int32)
            queries = lax.dynamic_slice_in_dim(floats, first_row, slots_all, 0)
            query_ids = lax.dynamic_slice_in_dim(member_ids, first_row, slots_all, 0)
            query_pos = first_row + jnp.arange(slots_all, dtype=jnp.int32)
            scores = jnp.dot(queries, floats.T, precision=lax.Precision.HIGHEST)
            return lax.optimization_barrier(jnp.max(masked_table(scores, query_ids, member_ids, query_pos, positions), axis=1))
        return lax.map(per_tile, jnp.arange(TILES, dtype=jnp.int32))
    results = lax.map(per_group, (buffers, tagged))
    results = results.reshape(GROUPS, TILES, GROUPS, CAP).transpose(2, 1, 0, 3).reshape(blocks, slots_all)
    return jnp.take_along_axis(results, placed, axis=1).reshape(ROWS)
```

```python
import functools

import jax
import jax.numpy as jnp
import numpy as np
from jax import lax
from jax.experimental import pallas as pl
from jax.experimental.pallas import tpu as pltpu
from jax.sharding import PartitionSpec as P

epsilon = 1e-06
AXES = ("grp", "tile")
SIDE, CORES = 4, 2
ROWS, WIDTH = 384, 1024
PAD = 16
CHUNK = 256
VMEM_BYTES = 56 * 1024 * 1024

OFFSETS = (
    (0, 0, 0),
    (1, 1, 0), (3, 0, 1), (0, 3, 0), (0, 0, 3),
    (0, 0, 2), (0, 2, 0), (2, 2, 0), (1, 1, 1), (2, 0, 1), (0, 3, 3),
)
ROUTES = {
    1: (0, (1, 1, 0)), 2: (0, (3, 0, 1)), 3: (0, (0, 3, 0)), 4: (0, (0, 0, 3)),
    5: (4, (0, 0, 3)), 6: (3, (0, 3, 0)), 7: (1, (1, 1, 0)),
    8: (1, (0, 0, 1)), 9: (2, (3, 0, 0)), 10: (4, (0, 3, 0)),
}
PAIRED = (0, 2, 3, 4, 5, 6, 10)
STAGES = (
    ((1, 0), (2, 0), (3, 0), (4, 0), (1, 2), (1, 3), (2, 3), (1, 4), (2, 4), (3, 4)),
    ((5, 0), (1, 5), (5, 2), (5, 3), (6, 0), (1, 6), (6, 2), (6, 4), (6, 5)),
    ((7, 0), (7, 2), (7, 3), (7, 4), (7, 5), (7, 6), (8, 5), (8, 6), (8, 10),
     (9, 0), (9, 2), (9, 3), (9, 4), (9, 10), (10, 0), (10, 2)),
)
RESULTS = 24


def device_index(x, y, z, core):
    return ((z % SIDE * CORES + core) * SIDE + y % SIDE) * SIDE + x % SIDE


def all_places():
    return [
        (x, y, z, core)
        for z in range(SIDE) for core in range(CORES) for y in range(SIDE) for x in range(SIDE)
    ]


def fetch(block, offset, other_core=False):
    pairs = []
    for x, y, z, core in all_places():
        source = device_index(
            x + offset[0], y + offset[1], z + offset[2], 1 - core if other_core else core
        )
        pairs.append((source, device_index(x, y, z, core)))
    return lax.ppermute(block, AXES, pairs)


def owner_table():
    table = np.zeros((SIDE**3 * CORES, RESULTS), np.int32)
    for x, y, z, core in all_places():
        here = device_index(x, y, z, core)
        for k, (dx, dy, dz) in enumerate(OFFSETS):
            table[here, k] = device_index(x + dx, y + dy, z + dz, core)
        for k, j in enumerate(PAIRED):
            dx, dy, dz = OFFSETS[j]
            table[here, len(OFFSETS) + k] = device_index(x + dx, y + dy, z + dz, 1 - core)
    return table


def prepare_kernel(rows_ref, keys_ref, block_ref):
    floats = rows_ref[...].astype(jnp.float32)
    scale = lax.rsqrt(jnp.sum(floats * floats, axis=-1, keepdims=True) + epsilon)
    block_ref[pl.ds(0, ROWS), :] = (floats * scale).astype(jnp.bfloat16)
    block_ref[pl.ds(ROWS, PAD), :] = jnp.zeros((PAD, WIDTH), jnp.bfloat16)
    block_ref[pl.ds(ROWS, PAD), pl.ds(0, ROWS)] = jnp.broadcast_to(
        keys_ref[...].astype(jnp.bfloat16), (PAD, ROWS)
    )


def prepare(rows, keys):
    return pl.pallas_call(
        prepare_kernel,
        out_shape=jax.ShapeDtypeStruct((ROWS + PAD, WIDTH), jnp.bfloat16),
        in_specs=[pl.BlockSpec(memory_space=pltpu.VMEM)] * 2,
        out_specs=pl.BlockSpec(memory_space=pltpu.VMEM),
        compiler_params=pltpu.CompilerParams(vmem_limit_bytes=VMEM_BYTES),
        name="prepare",
    )(rows, keys.astype(jnp.float32).reshape(1, ROWS))


def compare_kernel(own, other, steps, with_self, last, *refs):
    refs = list(refs)
    own_refs = {k: refs.pop(0) for k in own}
    other_refs = {k: refs.pop(0) for k in other}
    before_ref = refs.pop(0)
    owners_ref = refs.pop(0) if last else None
    out_ref = refs.pop(0)
    data, tags, row_best, col_best, row_key, col_key, sems = refs
    slot = {k: n for n, k in enumerate(own)}

    copies = {}
    for k in own:
        n = slot[k]
        parts = [
            (own_refs[k].at[pl.ds(0, ROWS)], data.at[n, pl.ds(0, ROWS)]),
            (own_refs[k].at[pl.ds(ROWS, PAD)], tags.at[n, 0]),
        ]
        if k in other:
            parts += [
                (other_refs[k].at[pl.ds(0, ROWS)], data.at[n, pl.ds(ROWS, ROWS)]),
                (other_refs[k].at[pl.ds(ROWS, PAD)], tags.at[n, 1]),
            ]
        copies[k] = [
            pltpu.make_async_copy(src, dst, sems.at[n, m]) for m, (src, dst) in enumerate(parts)
        ]
        for copy in copies[k]:
            copy.start()

    row_best[...] = jnp.full(row_best.shape, -1.0, jnp.float32)
    col_best[...] = jnp.full(col_best.shape, -1.0, jnp.float32)
    ready = set()

    def need(k):
        if k in ready:
            return
        ready.add(k)
        n = slot[k]
        for copy in copies[k]:
            copy.wait()
        first = tags[n, 0, pl.ds(0, 1), pl.ds(0, ROWS)].astype(jnp.float32)
        row_key[n] = jnp.broadcast_to(first, (128, ROWS)).T
        col_key[n, :, pl.ds(0, ROWS)] = jnp.broadcast_to(first, (8, ROWS))
        if k in other:
            second = tags[n, 1, pl.ds(0, 1), pl.ds(0, ROWS)].astype(jnp.float32)
            col_key[n, :, pl.ds(ROWS, ROWS)] = jnp.broadcast_to(second, (8, ROWS))

    def compare(i, j, same):
        for part in range(2 * ROWS // CHUNK):
            cols = pl.ds(part * CHUNK, CHUNK)
            scores = lax.dot_general(
                data[i, pl.ds(0, ROWS), :], data[j, cols, :],
                (((1,), (1,)), ((), ())), preferred_element_type=jnp.float32,
            )
            best = row_best[i]
            for half in range(CHUNK // 128):
                lanes = pl.ds(part * CHUNK + half * 128, 128)
                allowed = row_key[i] == col_key[j, pl.ds(0, 1), lanes]
                if same and part * CHUNK + half * 128 < ROWS:
                    rows_at = lax.broadcasted_iota(jnp.int32, (ROWS, 128), 0)
                    cols_at = lax.broadcasted_iota(jnp.int32, (ROWS, 128), 1)
                    allowed &= rows_at != cols_at + (part * CHUNK + half * 128)
                kept = jnp.where(allowed, scores[:, half * 128:(half + 1) * 128], -1.0)
                best = jnp.maximum(best, kept)
                col_best[j, :, lanes] = jnp.maximum(
                    col_best[j, :, lanes], jnp.max(kept.reshape(ROWS // 8, 8, 128), axis=0)
                )
            row_best[i] = best

    if with_self:
        need(0)
        compare(slot[0], slot[0], True)
    for i, j in steps:
        need(i)
        need(j)
        compare(slot[i], slot[j], False)

    if last:
        out_ref[...] = jnp.full(out_ref.shape, -1.0, jnp.float32)
    else:
        out_ref[...] = before_ref[...]
    for k in range(len(OFFSETS)):
        best = before_ref[pl.ds(k, 1), :]
        if k in own:
            by_row = jnp.max(row_best[slot[k]].T, axis=0, keepdims=True)
            by_col = jnp.max(col_best[slot[k], :, pl.ds(0, ROWS)], axis=0, keepdims=True)
            best = jnp.maximum(best, jnp.maximum(by_row, by_col))
        row = owners_ref[k] if last else k
        out_ref[pl.ds(row, 1), :] = best
    for n, k in enumerate(PAIRED):
        at = len(OFFSETS) + n
        best = before_ref[pl.ds(at, 1), :]
        if k in other:
            by_col = jnp.max(col_best[slot[k], :, pl.ds(ROWS, ROWS)], axis=0, keepdims=True)
            best = jnp.maximum(best, by_col)
        row = owners_ref[at] if last else at
        out_ref[pl.ds(row, 1), :] = best


def compare(blocks, others, steps, before, owners=None, with_self=False):
    own, other = [], []
    for i, j in ([(0, 0)] if with_self else []) + list(steps):
        for k in (j, i):
            if k not in own:
                own.append(k)
        if j not in other:
            other.append(j)
    last = owners is not None
    count = len(own)
    operands = [blocks[k] for k in own] + [others[k] for k in other] + [before]
    specs = [pl.BlockSpec(memory_space=pl.ANY)] * (len(own) + len(other))
    specs += [pl.BlockSpec(memory_space=pltpu.VMEM)]
    if last:
        operands.append(owners)
        specs.append(pl.BlockSpec(memory_space=pltpu.SMEM))
    rows_out = SIDE**3 * CORES if last else RESULTS
    pairs = len(steps) + int(with_self)
    return pl.pallas_call(
        functools.partial(compare_kernel, own, other, steps, with_self, last),
        out_shape=jax.ShapeDtypeStruct((rows_out, ROWS), jnp.float32),
        in_specs=specs,
        out_specs=pl.BlockSpec(memory_space=pltpu.VMEM),
        scratch_shapes=[
            pltpu.VMEM((count, 2 * ROWS, WIDTH), jnp.bfloat16),
            pltpu.VMEM((count, 2, PAD, WIDTH), jnp.bfloat16),
            pltpu.VMEM((count, ROWS, 128), jnp.float32),
            pltpu.VMEM((count, 8, 2 * ROWS), jnp.float32),
            pltpu.VMEM((count, ROWS, 128), jnp.float32),
            pltpu.VMEM((count, 8, 2 * ROWS), jnp.float32),
            pltpu.SemaphoreType.DMA((count, 4)),
        ],
        compiler_params=pltpu.CompilerParams(vmem_limit_bytes=VMEM_BYTES),
        cost_estimate=pl.CostEstimate(
            flops=pairs * 4 * ROWS * ROWS * WIDTH,
            bytes_accessed=(len(own) + len(other)) * ROWS * WIDTH * 2,
            transcendentals=0,
        ),
        name="compare",
    )(*operands)


def local(embeddings, row_group, row_cluster):
    keys = row_group * 2 + row_cluster
    blocks = {0: prepare(embeddings, keys)}
    others = {0: fetch(blocks[0], (0, 0, 0), other_core=True)}
    for k, (source, offset) in ROUTES.items():
        blocks[k] = fetch(blocks[source], offset)
    for k in PAIRED[1:]:
        others[k] = fetch(blocks[k], (0, 0, 0), other_core=True)
    here = lax.axis_index("grp") * (SIDE * SIDE) + lax.axis_index("tile")
    owners = lax.dynamic_index_in_dim(jnp.asarray(owner_table()), here, 0, keepdims=False)
    best = jnp.full((RESULTS, ROWS), -1.0, jnp.float32)
    best = compare(blocks, others, STAGES[0], best, with_self=True)
    best = compare(blocks, others, STAGES[1], best)
    outgoing = compare(blocks, others, STAGES[2], best, owners)
    arrived = lax.all_to_all(outgoing, AXES, split_axis=0, concat_axis=0, tiled=True)
    return jnp.max(arrived, axis=0)


def solution(mesh):
    placed = (P(AXES, None), P(AXES), P(AXES))
    return jax.shard_map(
        local, mesh=mesh, in_specs=placed, out_specs=P(AXES), check_vma=False
    )
```

```python
import functools

import jax
import jax.numpy as jnp
import numpy as np
from jax import lax
from jax.experimental import pallas as pl
from jax.experimental.pallas import tpu as pltpu
from jax.sharding import PartitionSpec as P

epsilon = 1e-06
AXES = ("grp", "tile")
SIDE, CORES = 4, 2
ROWS, WIDTH = 384, 1024
PAD = 16
CHUNK = 256
VMEM_BYTES = 16 * 1024 * 1024

OFFSETS = (
    (0, 0, 0),
    (1, 1, 0), (3, 0, 1), (0, 3, 0), (0, 0, 3),
    (0, 0, 2), (0, 2, 0), (2, 2, 0), (1, 1, 1), (2, 0, 1), (0, 3, 3),
)
ROUTES = {
    1: (0, (1, 1, 0)), 2: (0, (3, 0, 1)), 3: (0, (0, 3, 0)), 4: (0, (0, 0, 3)),
    5: (4, (0, 0, 3)), 6: (3, (0, 3, 0)), 7: (1, (1, 1, 0)),
    8: (1, (0, 0, 1)), 9: (2, (3, 0, 0)),
}
LAST = 10
LAST_ROUTES = ((4, (0, 3, 0)), (3, (0, 0, 3)))
PAIRED = (0, 2, 3, 4, 5, 6, 8, 9)
STAGES = (
    ((1, 0), (2, 0), (3, 0), (4, 0), (1, 2), (1, 3), (2, 3), (1, 4), (2, 4), (3, 4)),
    ((5, 0), (6, 0), (7, 0), (9, 0), (5, 2), (6, 2), (7, 2), (9, 2), (5, 3), (7, 3), (9, 3),
     (6, 4), (7, 4), (9, 4)),
    ((1, 5), (6, 5), (7, 5), (8, 5), (1, 6), (7, 6), (8, 6), (10, 0), (10, 2), (10, 8), (10, 9)),
)
RESULTS = len(OFFSETS) + len(PAIRED)


def device_index(x, y, z, core):
    return ((z % SIDE * CORES + core) * SIDE + y % SIDE) * SIDE + x % SIDE


def all_places():
    return [
        (x, y, z, core)
        for z in range(SIDE) for core in range(CORES) for y in range(SIDE) for x in range(SIDE)
    ]


def fetch(block, offsets, other_core=False):
    pairs = []
    for x, y, z, core in all_places():
        dx, dy, dz = offsets[core]
        source = device_index(x + dx, y + dy, z + dz, 1 - core if other_core else core)
        pairs.append((source, device_index(x, y, z, core)))
    return lax.ppermute(block, AXES, pairs)


def owner_table():
    table = np.zeros((SIDE**3 * CORES, RESULTS), np.int32)
    for x, y, z, core in all_places():
        here = device_index(x, y, z, core)
        for k, (dx, dy, dz) in enumerate(OFFSETS):
            table[here, k] = device_index(x + dx, y + dy, z + dz, core)
        for k, j in enumerate(PAIRED):
            dx, dy, dz = OFFSETS[j]
            table[here, len(OFFSETS) + k] = device_index(x + dx, y + dy, z + dz, 1 - core)
    return table


def prepare_kernel(rows_ref, keys_ref, block_ref):
    floats = rows_ref[...].astype(jnp.float32)
    scale = lax.rsqrt(jnp.sum(floats * floats, axis=-1, keepdims=True) + epsilon)
    block_ref[pl.ds(0, ROWS), :] = (floats * scale).astype(jnp.bfloat16)
    block_ref[pl.ds(ROWS, PAD), :] = jnp.zeros((PAD, WIDTH), jnp.bfloat16)
    block_ref[pl.ds(ROWS, PAD), pl.ds(0, ROWS)] = jnp.broadcast_to(
        keys_ref[...].astype(jnp.bfloat16), (PAD, ROWS)
    )


def prepare(rows, keys):
    return pl.pallas_call(
        prepare_kernel,
        out_shape=jax.ShapeDtypeStruct((ROWS + PAD, WIDTH), jnp.bfloat16),
        in_specs=[pl.BlockSpec(memory_space=pltpu.VMEM)] * 2,
        out_specs=pl.BlockSpec(memory_space=pltpu.VMEM),
        compiler_params=pltpu.CompilerParams(vmem_limit_bytes=VMEM_BYTES),
        name="prepare",
    )(rows, keys.astype(jnp.float32).reshape(1, ROWS))


def compare_kernel(own, other, steps, with_self, merge, last, *refs):
    refs = list(refs)
    own_refs = {k: refs.pop(0) for k in own}
    other_refs = {k: refs.pop(0) for k in other}
    before_ref = refs.pop(0) if merge else None
    owners_ref = refs.pop(0) if last else None
    out_ref = refs.pop(0)
    row_best, col_best, row_key = refs
    slot = {k: n for n, k in enumerate(own)}
    left = {i for i, _ in steps} | ({0} if with_self else set())

    col_best[...] = jnp.full(col_best.shape, -1.0, jnp.float32)

    def keys_of(ref):
        return ref[pl.ds(ROWS, PAD), pl.ds(0, ROWS)][0:1].astype(jnp.float32)

    for k in left:
        row_key[slot[k]] = jnp.broadcast_to(keys_of(own_refs[k]), (128, ROWS)).T
        row_best[slot[k]] = jnp.full((ROWS, 128), -1.0, jnp.float32)

    def pieces(j, part):
        out = []
        for at in range(part * CHUNK, (part + 1) * CHUNK, 128):
            rows = pl.ds(at % ROWS, 128)
            out.append((own_refs if at < ROWS else other_refs)[j][rows, :])
        return jnp.concatenate(out, axis=0)

    def compare(i, j, part, same):
        n, m = slot[i], slot[j]
        scores = lax.dot_general(
            own_refs[i][pl.ds(0, ROWS), :], pieces(j, part),
            (((1,), (1,)), ((), ())), preferred_element_type=jnp.float32,
        )
        best = row_best[n]
        for half in range(CHUNK // 128):
            at = part * CHUNK + half * 128
            lanes = pl.ds(at, 128)
            keys = keys_of((own_refs if at < ROWS else other_refs)[j])
            allowed = row_key[n] == keys[:, at % ROWS:at % ROWS + 128]
            if same and at < ROWS:
                rows_at = lax.broadcasted_iota(jnp.int32, (ROWS, 128), 0)
                cols_at = lax.broadcasted_iota(jnp.int32, (ROWS, 128), 1)
                allowed &= rows_at != cols_at + at
            kept = jnp.where(allowed, scores[:, half * 128:(half + 1) * 128], -1.0)
            best = jnp.maximum(best, kept)
            col_best[m, :, lanes] = jnp.maximum(
                col_best[m, :, lanes], jnp.max(kept.reshape(ROWS // 8, 8, 128), axis=0)
            )
        row_best[n] = best

    for part in range(2 * ROWS // CHUNK):
        if with_self:
            compare(0, 0, part, True)
        for i, j in steps:
            compare(i, j, part, False)

    def turned(block):
        rows_at = lax.broadcasted_iota(jnp.int32, (128, 128), 0)
        cols_at = lax.broadcasted_iota(jnp.int32, (128, 128), 1)
        return lax.dot_general(
            (rows_at == cols_at).astype(jnp.float32), block, (((1,), (1,)), ((), ())),
            preferred_element_type=jnp.float32, precision=lax.Precision.HIGHEST,
        )

    if last:
        out_ref[...] = jnp.full(out_ref.shape, -1.0, jnp.float32)
    for k in range(RESULTS):
        best = before_ref[pl.ds(k, 1), :] if merge else jnp.full((1, ROWS), -1.0, jnp.float32)
        if k < len(OFFSETS):
            if k in left:
                best = jnp.maximum(best, jnp.max(turned(row_best[slot[k]]), axis=0, keepdims=True))
            if k in other:
                best = jnp.maximum(
                    best, jnp.max(col_best[slot[k], :, pl.ds(0, ROWS)], axis=0, keepdims=True)
                )
        elif PAIRED[k - len(OFFSETS)] in other:
            half = col_best[slot[PAIRED[k - len(OFFSETS)]], :, pl.ds(ROWS, ROWS)]
            best = jnp.maximum(best, jnp.max(half, axis=0, keepdims=True))
        out_ref[pl.ds(owners_ref[k] if last else k, 1), :] = best


def compare(blocks, others, steps, before, owners=None, with_self=False):
    own, other = [], []
    for i, j in ([(0, 0)] if with_self else []) + list(steps):
        for k in (j, i):
            if k not in own:
                own.append(k)
        if j not in other:
            other.append(j)
    last = owners is not None
    count = len(own)
    operands = [blocks[k] for k in own] + [others[k] for k in other]
    if before is not None:
        operands.append(before)
    specs = [pl.BlockSpec(memory_space=pltpu.VMEM)] * len(operands)
    if last:
        operands.append(owners)
        specs.append(pl.BlockSpec(memory_space=pltpu.SMEM))
    rows_out = SIDE**3 * CORES if last else RESULTS
    pairs = len(steps) + int(with_self)
    return pl.pallas_call(
        functools.partial(compare_kernel, own, other, steps, with_self, before is not None, last),
        out_shape=jax.ShapeDtypeStruct((rows_out, ROWS), jnp.float32),
        in_specs=specs,
        out_specs=pl.BlockSpec(memory_space=pltpu.VMEM),
        scratch_shapes=[
            pltpu.VMEM((count, ROWS, 128), jnp.float32),
            pltpu.VMEM((count, 8, 2 * ROWS), jnp.float32),
            pltpu.VMEM((count, ROWS, 128), jnp.float32),
        ],
        compiler_params=pltpu.CompilerParams(vmem_limit_bytes=VMEM_BYTES),
        cost_estimate=pl.CostEstimate(
            flops=pairs * ROWS * ROWS * WIDTH // 2, bytes_accessed=0, transcendentals=0
        ),
        name="compare",
    )(*operands)


def after(block, *earlier):
    return lax.optimization_barrier((block, *earlier))[0]


def local(embeddings, row_group, row_cluster):
    keys = row_group * 2 + row_cluster
    first_core = lax.axis_index("grp") % CORES == 0
    here = lax.axis_index("grp") * (SIDE * SIDE) + lax.axis_index("tile")
    owners = lax.dynamic_index_in_dim(jnp.asarray(owner_table()), here, 0, keepdims=False)
    keys, first_core, owners = lax.optimization_barrier((keys, first_core, owners))
    blocks = {0: prepare(embeddings, keys)}
    others = {}

    def bring(k, *earlier):
        source, offset = ROUTES[k]
        block = after(blocks[source], *earlier) if earlier else blocks[source]
        blocks[k] = fetch(block, (offset, offset))

    def bring_last(*earlier):
        (first, offset), (second, other_offset) = LAST_ROUTES
        block = lax.select(first_core, blocks[first], blocks[second])
        blocks[LAST] = fetch(after(block, *earlier), (offset, other_offset))

    def swap(k, *earlier):
        block = after(blocks[k], *earlier) if earlier else blocks[k]
        others[k] = fetch(block, ((0, 0, 0), (0, 0, 0)), other_core=True)

    swap(0)
    for k in (1, 2):
        bring(k)
    for k in (3, 4):
        bring(k, others[0])
    for k in (4, 3, 2):
        swap(k)
    for k in (7, 8, 9, 5, 6):
        bring(k, others[0])
    best = compare(blocks, others, STAGES[0], None, with_self=True)
    bring_last(best)
    for k in (5, 6, 8, 9):
        swap(k, best)
    best = compare(blocks, others, STAGES[1], best)
    outgoing = compare(blocks, others, STAGES[2], best, owners)
    arrived = lax.all_to_all(outgoing, AXES, split_axis=0, concat_axis=0, tiled=True)
    return jnp.max(arrived, axis=0)


def solution(mesh):
    placed = (P(AXES, None), P(AXES), P(AXES))
    return jax.shard_map(
        local, mesh=mesh, in_specs=placed, out_specs=P(AXES), check_vma=False
    )
```
